32 devices in a mesh: group: 2 (over y), sky: 4 (over z), visit: 2 (over x), band: 2 (over core).
Axes of the slice: x: 2, y: 2, z: 4, core: 2. Of those that a mesh axis runs over, the one named last changes fastest.
Arguments:
- raw_tiles: bfloat16 [16, 32, 128, 128], P(('group', 'visit', 'band'), 'sky'), parts along dimension 0, may hold values from -6 to 6
- pixel_offsets: int32 [16, 32, 2], P(('group', 'visit', 'band'), 'sky'), parts along dimension 0, may hold values from -1 to 1
- shift_entry_index: int32 [16, 32], P(('group', 'visit', 'band'), 'sky'), parts along dimension 0, may hold values from 0 to 15
- shift_table: float32 [16, 2], replicated, may hold values from 0 to 1
- tile_routes: int32 [16, 32], P(('group', 'visit', 'band'), 'sky'), parts along dimension 0, may hold values from 0 to 31, as said below
- bad_pixels: int32 [16, 32, 32], P('group', 'sky'), parts along dimension 0, may hold values from 0 to 16383, as said below
- basis_kernels: bfloat16 [4, 33, 33], replicated, may hold values from -0.5 to 0.5
- basis_choice: int32 [16, 32], P(('group', 'visit', 'band'), 'sky'), parts along dimension 0, may hold values from 0 to 15
- coef_table: float32 [16, 4], replicated, may hold values from -4 to 4
Outputs:
- difference: bfloat16 [16, 512, 1024], P(('group', 'visit', 'band'), 'sky'), parts along dimension 0
The draws below stay inside these ranges and needn't reach their ends.
There are 2 independent parts, one for each index of `group`. The reference program is written for one: setup_inputs(seed, part) draws one part's arguments, and reference() takes and returns one part's arrays. A program takes and returns all parts, laid end to end along the dimension named above; an argument that names none is the same for every part. Nothing has to cross between parts.
Inputs may be any that keep to these rules, and one draw needn't show every extreme that they name: `tile_routes`: for every visit, each of the 32 slab tiles is named by exactly one source tile. Within each aligned block of 2 visits, the source tiles i with one value of i // 8 name at most 5 slab tiles t with one value of t // 8, and exactly 5 for some value. `bad_pixels`: an entry names the pixel at row r and column c of the slab tile as r * 128 + c. For one slab tile, the entries of all visits together are distinct.
All inputs are finite; a program needn't handle non-finite values.
Results may differ from the reference program's by a relative error of at most 0.018.
Values may be sent and summed in bfloat16 or wider, within the bound.
A program may use at most 128 MiB of HBM per device.

```python
import jax
import jax.numpy as jnp
from jax import lax

TILE = 128
KS = 33
NB = 4
SHIFT_ENTRIES = 16
NCOEF = 16
VIS_DEV = 2
TCOLS = 8
NBAD = 32
VISITS = 8
TILES = 32
N_SKY = 4


def route_block(key):
    patches = TILES // TCOLS
    pooled_width = VIS_DEV * TCOLS
    capacity = (pooled_width + patches - 1) // patches + 1
    sub_keys = jax.random.split(key, 6)
    sigma_order = jax.random.permutation(sub_keys[0], patches).astype(jnp.int32)
    tau_order = jax.random.permutation(sub_keys[1], patches).astype(jnp.int32)
    class_offsets = jax.random.permutation(sub_keys[2], patches).astype(jnp.int32)
    slot_order = jax.random.permutation(sub_keys[3], pooled_width).astype(jnp.int32)
    seat_draw = jax.random.permutation(sub_keys[4], (patches - 1) * capacity).astype(jnp.int32)
    seat_padded = jnp.concatenate([seat_draw, jnp.zeros((pooled_width,), jnp.int32)])
    positions = jnp.zeros((pooled_width,), jnp.int32).at[slot_order].set(jnp.arange(pooled_width, dtype=jnp.int32))
    seat_index = jnp.clip(positions - capacity, 0, pooled_width - 1)
    classes = jnp.where(positions < capacity, 0, 1 + seat_padded[seat_index] // capacity)
    owners = tau_order[(sigma_order[:, None] + class_offsets[classes][None, :]) % patches]
    owner_grid = owners.reshape(patches, VIS_DEV, TCOLS).transpose(1, 0, 2)
    scores = jax.random.randint(sub_keys[5], (VIS_DEV, patches, TCOLS), 0, 1048576) * TCOLS + jnp.arange(TCOLS, dtype=jnp.int32)
    arrival = jnp.argsort(scores, axis=-1, stable=True).astype(jnp.int32)
    selected_entries = jnp.take_along_axis(arrival, owner_grid, axis=1)
    return (owner_grid * TCOLS + selected_entries).reshape(VIS_DEV, patches * TCOLS).astype(jnp.int32)


def draw_tile_routes(key, part):
    shard_keys = jax.random.split(jax.random.fold_in(key, 7), VISITS // VIS_DEV)
    return jax.vmap(route_block)(shard_keys).reshape(VISITS, TILES)


def draw_bad_pixels(key, part):
    tile_keys = jax.random.split(jax.random.fold_in(key, 11), TILES)

    def one_order(tile_key):
        return jax.random.permutation(tile_key, TILE * TILE).astype(jnp.int32)
    orders = jax.vmap(one_order)(tile_keys)
    selected_entries = orders[:, :VISITS * NBAD].reshape(TILES, VISITS, NBAD)
    return jnp.transpose(selected_entries, (1, 0, 2)).astype(jnp.int32)


def plant(entries, stream_key, low, high):
    longest = entries.shape.index(max(entries.shape))
    spots = []
    for shift in (0, 1):
        where = [jax.random.randint(jax.random.fold_in(stream_key, axis), (), 0, length) for axis, length in enumerate(entries.shape)]
        where[longest] = (where[longest] + shift) % entries.shape[longest]
        spots.append(tuple(where))
    return entries.at[spots[0]].set(low).at[spots[1]].set(high)


def levels(key, shape, pieces, low, top_value):
    factor_of = 1.0
    for dim, shards_of in pieces:
        steps = jax.random.uniform(jax.random.fold_in(jax.random.fold_in(key, 6), dim), (shards_of,), jnp.float32, low / len(pieces), top_value / len(pieces))
        factor_of = factor_of * jnp.repeat(jnp.exp(steps), shape[dim] // shards_of).reshape((-1,) + (1,) * (len(shape) - 1 - dim))
    return factor_of


def gaussian(stream_key, extent, scale, bound, shards=(), kind=jnp.bfloat16):
    level = levels(stream_key, extent, shards, -0.22, 0.18) if shards else 1.0
    result = jax.random.normal(stream_key, extent, jnp.float32) * scale * level
    return jnp.minimum(jnp.maximum(result, -bound), bound).astype(kind)


def setup_inputs(seed: int = 0, part: int = 0) -> dict:
    splits = jax.random.split(jax.random.key(seed), 10)
    part_keys = jax.random.split(jax.random.fold_in(splits[9], part), 10)
    return {
        "raw_tiles": gaussian(part_keys[0], (VISITS, TILES, TILE, TILE), 1.0, 6.0, ((0, 4), (1, 4))),
        "pixel_offsets": plant(jax.random.randint(part_keys[1], (VISITS, TILES, 2), -1, 2), jax.random.fold_in(part_keys[1], 1), -1, 1).astype(jnp.int32),
        "shift_entry_index": plant(jax.random.randint(part_keys[2], (VISITS, TILES), 0, SHIFT_ENTRIES), jax.random.fold_in(part_keys[2], 1), 0, SHIFT_ENTRIES - 1).astype(jnp.int32),
        "shift_table": jnp.clip(jax.random.uniform(splits[3], (SHIFT_ENTRIES, 2), jnp.float32, 0.0, 1.0), 0.0, 1.0),
        "tile_routes": draw_tile_routes(jax.random.fold_in(jax.random.fold_in(splits[9], part), 71), part),
        "bad_pixels": draw_bad_pixels(jax.random.fold_in(jax.random.fold_in(splits[9], part), 71), part),
        "basis_kernels": gaussian(splits[6], (NB, KS, KS), (KS * KS // 8) ** -0.5, 0.5),
        "basis_choice": plant(jax.random.randint(part_keys[7], (VISITS, TILES), 0, NCOEF), jax.random.fold_in(part_keys[7], 1), 0, NCOEF - 1).astype(jnp.int32),
        "coef_table": gaussian(splits[8], (NCOEF, NB), 1.0, 4.0, (), jnp.float32),
    }


def lanczos(offset):
    return jnp.where(jnp.abs(offset) < 3.0, jnp.sinc(offset) * jnp.sinc(offset / 3.0), 0.0)


def to_image(tiles):
    return tiles.reshape(N_SKY, TCOLS, TILE, TILE).transpose(0, 2, 1, 3).reshape(TILE * N_SKY, TCOLS * TILE)


def one_visit(raw_tile, offsets, selected_entries, routes, listed, shift_table):
    fraction = shift_table[selected_entries]
    shifts = offsets.astype(jnp.float32) + fraction
    target_positions = jnp.arange(TILE).astype(jnp.float32)
    spacing = target_positions[:, None] - target_positions[None, :]
    row_weights = lanczos(spacing[None] - shifts[:, 0, None, None]).astype(jnp.bfloat16)
    col_weights = lanczos(spacing[None] - shifts[:, 1, None, None]).astype(jnp.bfloat16)
    halfway = jnp.einsum("tap,tpq->taq", row_weights.astype(jnp.float32), raw_tile.astype(jnp.float32), precision=lax.Precision.HIGHEST).astype(jnp.bfloat16)
    warped = jnp.einsum("taq,tbq->tab", halfway.astype(jnp.float32), col_weights.astype(jnp.float32), precision=lax.Precision.HIGHEST).astype(jnp.bfloat16)
    placed = jnp.zeros_like(warped).at[routes].set(warped)
    indices = jnp.arange(TILE).astype(jnp.int32)
    row_match_count = (listed[:, None, :] // TILE == indices[None, :, None]).astype(jnp.float32)
    column_match_count = (listed[:, None, :] % TILE == indices[None, :, None]).astype(jnp.float32)
    marked_pixels = jnp.einsum("svw,srw->svr", row_match_count, column_match_count, precision=lax.Precision.HIGHEST)
    return to_image(placed), to_image(marked_pixels).astype(jnp.bfloat16)


def reference(raw_tiles, pixel_offsets, shift_entry_index, shift_table, tile_routes, bad_pixels, basis_kernels, basis_choice, coef_table):
    def visit_step(inputs):
        raw_tile, offsets, selected_entries, routes, listed = inputs
        return one_visit(raw_tile, offsets, selected_entries, routes, listed, shift_table)

    slab_images, marked_pixels = lax.map(visit_step, (raw_tiles, pixel_offsets, shift_entry_index, tile_routes, bad_pixels))
    valid_pixel_mask = 1.0 - marked_pixels.astype(jnp.float32)
    values = slab_images.astype(jnp.float32)
    summed = jnp.sum(valid_pixel_mask * values, axis=0)
    tallies = jnp.sum(valid_pixel_mask, axis=0)
    highest = jnp.max(jnp.where(valid_pixel_mask > 0.5, values, -jnp.inf), axis=0)
    lowest = jnp.min(jnp.where(valid_pixel_mask > 0.5, values, jnp.inf), axis=0)
    coadded = ((summed - highest - lowest) / (tallies - 2.0)).astype(jnp.bfloat16)
    margin = KS // 2
    filtered = lax.conv_general_dilated(coadded.astype(jnp.float32)[None, None], basis_kernels.astype(jnp.float32)[:, None], (1, 1), ((margin, margin), (margin, margin)), precision=lax.Precision.HIGHEST)[0].astype(jnp.bfloat16)
    mixture = coef_table[basis_choice].reshape(VISITS, N_SKY, TCOLS, NB)
    basis_planes = filtered.astype(jnp.float32).reshape(NB, N_SKY, TILE, TCOLS, TILE)
    template = jnp.einsum("vskb,bsakc->vsakc", mixture, basis_planes, precision=lax.Precision.HIGHEST).reshape(VISITS, TILE * N_SKY, TCOLS * TILE)
    return ((values - template) * valid_pixel_mask).astype(jnp.bfloat16)
```

```python
import jax
import jax.numpy as jnp
from jax import lax
from jax.sharding import PartitionSpec as P


def with_halo(block, sides, width):
    for axis, dim in sides:
        count = lax.axis_size(axis)
        forward = [(i, i + 1) for i in range(count - 1)]
        backward = [(target, source) for source, target in forward]
        low = lax.ppermute(
            lax.slice_in_dim(block, block.shape[dim] - width, None, axis=dim), axis, forward
        )
        high = lax.ppermute(lax.slice_in_dim(block, 0, width, axis=dim), axis, backward)
        block = jnp.concatenate([low, block, high], axis=dim)
    return block


def lanczos(offset):
    return jnp.where(jnp.abs(offset) < 3.0, jnp.sinc(offset) * jnp.sinc(offset / 3.0), 0.0)


def tiles_to_image(tiles):
    visit_count, tile_cols, tile_side = (tiles.shape[0], tiles.shape[1], tiles.shape[2])
    return jnp.transpose(tiles, (0, 2, 1, 3)).reshape(visit_count, tile_side, tile_cols * tile_side)


def hit_planes(listed, tile_side):
    indices = jnp.arange(tile_side)
    row_match_count = (listed[..., None, :] // tile_side == indices[:, None]).astype(jnp.bfloat16)
    column_match_count = (listed[..., None, :] % tile_side == indices[:, None]).astype(jnp.bfloat16)
    return jnp.einsum(
        "...am,...bm->...ab",
        row_match_count,
        column_match_count,
        preferred_element_type=jnp.float32,
    )


def warp_tiles(raw_tiles, pixel_offsets, shift_entry_index, shift_table):
    entries = shift_table.shape[0]
    tile_side = raw_tiles.shape[-1]
    selected_entries = (shift_entry_index[..., None] == jnp.arange(entries)).astype(jnp.float32)
    fraction = jnp.sum(selected_entries[..., None] * shift_table, axis=-2)
    shifts = pixel_offsets.astype(jnp.float32) + fraction
    target_positions = jnp.arange(tile_side).astype(jnp.float32)
    spacing = target_positions[:, None] - target_positions[None, :]
    row_weights = lanczos(spacing - shifts[..., 0, None, None]).astype(jnp.bfloat16)
    col_weights = lanczos(spacing - shifts[..., 1, None, None]).astype(jnp.bfloat16)
    halfway = jnp.einsum(
        "vtap,vtpq->vtaq", row_weights, raw_tiles, preferred_element_type=jnp.float32
    ).astype(jnp.bfloat16)
    return jnp.einsum(
        "vtaq,vtbq->vtab", halfway, col_weights, preferred_element_type=jnp.float32
    ).astype(jnp.bfloat16)


def banded_filter(padded, kernels, tile_side, tile_cols):
    kernel_side = kernels.shape[-1]
    window_width = tile_side + kernel_side - 1
    windows = jnp.stack(
        [padded[:, j * tile_side : j * tile_side + window_width] for j in range(tile_cols)]
    )
    lead = kernels.shape[:2]
    padded_rows = jnp.pad(kernels, ((0, 0), (0, 0), (0, window_width + 1 - kernel_side)))
    repeated = jnp.broadcast_to(
        padded_rows[:, :, None, :], lead + (tile_side, window_width + 1)
    ).reshape(lead + (tile_side * (window_width + 1),))
    bands = repeated[:, :, : tile_side * window_width].reshape(lead + (tile_side, window_width))

    def one_tile(window):
        shifted = jnp.stack([window[dy : dy + tile_side] for dy in range(kernel_side)], axis=1)
        return jnp.einsum("adx,bdcx->bac", shifted, bands, preferred_element_type=jnp.float32)

    result = lax.map(one_tile, windows)
    basis_count = kernels.shape[0]
    return (
        jnp.transpose(result, (1, 2, 0, 3))
        .reshape(basis_count, tile_side, tile_cols * tile_side)
        .astype(jnp.bfloat16)
    )


def on_device(
    raw_tiles,
    pixel_offsets,
    shift_entry_index,
    shift_table,
    tile_routes,
    bad_pixels,
    basis_kernels,
    basis_choice,
    coef_table,
):
    visit_count, tile_cols, tile_side = (raw_tiles.shape[0], raw_tiles.shape[1], raw_tiles.shape[2])
    tile_area = tile_side * tile_side
    patches = lax.axis_size("sky")
    capacity = (visit_count * tile_cols + patches - 1) // patches + 1
    seat_count = patches * capacity
    warped = warp_tiles(raw_tiles, pixel_offsets, shift_entry_index, shift_table)
    owners = tile_routes // tile_cols
    slot_ids = tile_routes % tile_cols
    before = jnp.arange(tile_cols)[None, :] < jnp.arange(tile_cols)[:, None]
    shared = owners[:, None, :] == owners[:, :, None]
    queue_rank = jnp.sum(shared & before[None], axis=2)
    seat_ids = owners * capacity + queue_rank
    layout = seat_ids[:, None, :] == jnp.arange(seat_count)[None, :, None]
    outgoing = jnp.einsum(
        "vsk,vkx->vsx",
        layout.astype(jnp.bfloat16),
        warped.reshape(visit_count, tile_cols, tile_area),
        preferred_element_type=jnp.float32,
    ).astype(jnp.bfloat16)
    labels = (jnp.sum(jnp.where(layout, slot_ids[:, None, :] + 1, 0), axis=2) - 1).astype(
        jnp.bfloat16
    )
    arrived, arrived_labels = (
        lax.all_to_all(
            outgoing.reshape(visit_count, patches, capacity * tile_area),
            "sky",
            split_axis=1,
            concat_axis=1,
            tiled=True,
        ),
        lax.all_to_all(
            labels.reshape(visit_count, patches, capacity),
            "sky",
            split_axis=1,
            concat_axis=1,
            tiled=True,
        ),
    )
    landing = (
        arrived_labels.astype(jnp.float32).reshape(visit_count, seat_count)[:, None, :]
        == jnp.arange(tile_cols).astype(jnp.float32)[None, :, None]
    )
    placed = jnp.einsum(
        "vks,vsx->vkx",
        landing.astype(jnp.bfloat16),
        arrived.reshape(visit_count, seat_count, tile_area),
        preferred_element_type=jnp.float32,
    ).astype(jnp.bfloat16)
    slab_image = tiles_to_image(placed.reshape(visit_count, tile_cols, tile_side, tile_side))
    shard_index = lax.axis_index(("visit", "band"))
    visit_total = bad_pixels.shape[0]
    listed_count = bad_pixels.shape[2]
    own_listed = lax.dynamic_slice_in_dim(bad_pixels, shard_index * visit_count, visit_count, 0)
    own_flags = tiles_to_image(hit_planes(own_listed, tile_side))
    valid_pixel_mask = 1.0 - own_flags
    all_listed = jnp.transpose(bad_pixels, (1, 0, 2)).reshape(
        1, tile_cols, visit_total * listed_count
    )
    all_flags = tiles_to_image(hit_planes(all_listed, tile_side))[0]
    tallies = visit_total - all_flags
    values = slab_image.astype(jnp.float32)
    partial_sums = jnp.sum(valid_pixel_mask * values, axis=0)
    partial_high = jnp.max(jnp.where(valid_pixel_mask > 0.5, slab_image, -jnp.inf), axis=0)
    partial_low = jnp.min(jnp.where(valid_pixel_mask > 0.5, slab_image, jnp.inf), axis=0)
    summed = lax.psum(partial_sums.astype(jnp.bfloat16), ("visit", "band")).astype(jnp.float32)
    highest = lax.pmax(partial_high, ("visit", "band"))
    lowest = lax.pmin(partial_low, ("visit", "band"))
    coadded = (
        (summed - highest.astype(jnp.float32) - lowest.astype(jnp.float32)) / (tallies - 2.0)
    ).astype(jnp.bfloat16)
    margin = basis_kernels.shape[-1] // 2
    padded = with_halo(coadded, (("sky", 0),), margin)
    padded = jnp.pad(padded, ((0, 0), (margin, margin)))
    per_device = basis_kernels.shape[0] // lax.axis_size("visit")
    own_kernels = lax.dynamic_slice_in_dim(
        basis_kernels, lax.axis_index("visit") * per_device, per_device, 0
    )
    filtered = lax.all_gather(
        banded_filter(padded, own_kernels, tile_side, tile_cols), "visit", axis=0, tiled=True
    )
    entries = coef_table.shape[0]
    picks = (basis_choice[..., None] == jnp.arange(entries)).astype(jnp.float32)
    mixture = jnp.sum(picks[..., None] * coef_table, axis=2)
    basis_count = basis_kernels.shape[0]
    basis_planes = filtered.astype(jnp.float32).reshape(
        basis_count, tile_side, tile_cols, tile_side
    )
    template = jnp.einsum(
        "vkb,bakc->vakc", mixture, basis_planes, precision=lax.Precision.HIGHEST
    ).reshape(visit_count, tile_side, tile_cols * tile_side)
    return ((values - template) * valid_pixel_mask).astype(jnp.bfloat16)


def solution(mesh):
    return jax.shard_map(
        on_device,
        mesh=mesh,
        in_specs=(
            P(("group", "visit", "band"), "sky", None, None),
            P(("group", "visit", "band"), "sky", None),
            P(("group", "visit", "band"), "sky"),
            P(),
            P(("group", "visit", "band"), "sky"),
            P("group", "sky", None),
            P(),
            P(("group", "visit", "band"), "sky"),
            P(),
        ),
        out_specs=P(("group", "visit", "band"), "sky", None),
        check_vma=False,
    )
```

```python
import functools

import jax
import jax.numpy as jnp
from jax import lax
from jax.experimental import pallas as pl
from jax.experimental.pallas import tpu as pltpu
from jax.sharding import PartitionSpec as P


def lanczos(offset):
    return jnp.where(jnp.abs(offset) < 3.0, jnp.sinc(offset) * jnp.sinc(offset / 3.0), 0.0)


def hit_planes(listed, tile_side):
    indices = jnp.arange(tile_side)
    row_match_count = (listed[..., None, :] // tile_side == indices[:, None]).astype(jnp.bfloat16)
    column_match_count = (listed[..., None, :] % tile_side == indices[:, None]).astype(jnp.bfloat16)
    return jnp.einsum(
        "...am,...bm->...ab",
        row_match_count,
        column_match_count,
        preferred_element_type=jnp.float32,
    )


def warp_tiles(raw_tiles, pixel_offsets, shift_entry_index, shift_table):
    entries = shift_table.shape[0]
    tile_side = raw_tiles.shape[-1]
    selected_entries = (shift_entry_index[..., None] == jnp.arange(entries)).astype(jnp.float32)
    fraction = jnp.sum(selected_entries[..., None] * shift_table, axis=-2)
    shifts = pixel_offsets.astype(jnp.float32) + fraction
    target_positions = jnp.arange(tile_side).astype(jnp.float32)
    spacing = target_positions[:, None] - target_positions[None, :]
    row_weights = lanczos(spacing - shifts[..., 0, None, None]).astype(jnp.bfloat16)
    col_weights = lanczos(spacing - shifts[..., 1, None, None]).astype(jnp.bfloat16)
    halfway = jnp.einsum(
        "vtap,vtpq->vtaq", row_weights, raw_tiles, preferred_element_type=jnp.float32
    ).astype(jnp.bfloat16)
    return jnp.einsum(
        "vtaq,vtbq->vtab", halfway, col_weights, preferred_element_type=jnp.float32
    ).astype(jnp.bfloat16)


MESH = pl.DeviceIdType.MESH


def coadd_kernel(
    sizes, margin, sum_ref, high_ref, low_ref, tally_ref, out_ref,
    got, full, sent_parts, got_parts, sent_rows, got_rows, sent_edge, got_edge,
):
    visits, bands, patches = sizes
    n = visits * bands
    tiles, rows, lanes = sum_ref.shape
    chunk = rows // n
    me = lax.axis_index("visit") * bands + lax.axis_index("band")
    sky = lax.axis_index("sky")
    has_low, has_high = sky > 0, sky < patches - 1

    def place(k):
        peer = lax.rem(me + k, n)
        return peer, {"visit": peer // bands, "band": lax.rem(peer, bands)}

    barrier = pltpu.get_barrier_semaphore()
    for k in range(1, n):
        pl.semaphore_signal(barrier, inc=1, device_id=place(k)[1], device_id_type=MESH)

    @pl.when(has_low)
    def _():
        pl.semaphore_signal(barrier, inc=1, device_id={"sky": sky - 1}, device_id_type=MESH)

    @pl.when(has_high)
    def _():
        pl.semaphore_signal(barrier, inc=1, device_id={"sky": sky + 1}, device_id_type=MESH)

    neighbours = (sky + patches - 1) // patches + (2 * patches - 2 - sky) // patches
    pl.semaphore_wait(barrier, n - 1 + neighbours)

    parts = (sum_ref, high_ref, low_ref)
    copies = []
    for k in range(1, n):
        peer, where = place(k)
        peer_rows = pl.ds(pl.multiple_of(peer * chunk, chunk), chunk)
        for i, part in enumerate(parts):
            copy = pltpu.make_async_remote_copy(
                src_ref=part.at[:, peer_rows],
                dst_ref=got.at[k - 1, i],
                send_sem=sent_parts.at[k - 1, i],
                recv_sem=got_parts.at[k - 1, i],
                device_id=where,
                device_id_type=MESH,
            )
            copy.start()
            copies.append(copy)

    @pl.when(jnp.logical_not(has_low))
    def _():
        full[:, :margin] = jnp.zeros((tiles, margin, lanes), full.dtype)

    @pl.when(jnp.logical_not(has_high))
    def _():
        full[:, rows + margin :] = jnp.zeros((tiles, margin, lanes), full.dtype)

    own_rows = pl.ds(pl.multiple_of(me * chunk, chunk), chunk)
    total, high, low = (part[:, own_rows].astype(jnp.float32) for part in parts)
    for copy in copies:
        copy.wait_recv()
    for k in range(n - 1):
        total += got[k, 0].astype(jnp.float32)
        high = jnp.maximum(high, got[k, 1].astype(jnp.float32))
        low = jnp.minimum(low, got[k, 2].astype(jnp.float32))
    count = tally_ref[:, own_rows].astype(jnp.float32)
    full_rows = pl.ds(pl.multiple_of(margin + me * chunk, 16), chunk)
    full[:, full_rows] = ((total - high - low) / (count - 2.0)).astype(full.dtype)

    shares = []
    for k in range(1, n):
        copy = pltpu.make_async_remote_copy(
            src_ref=full.at[:, full_rows],
            dst_ref=full.at[:, full_rows],
            send_sem=sent_rows.at[k - 1],
            recv_sem=got_rows.at[k - 1],
            device_id=place(k)[1],
            device_id_type=MESH,
        )
        copy.start()
        shares.append(copy)
    for copy in copies:
        copy.wait_send()
    for copy in shares:
        copy.wait_recv()

    up = pltpu.make_async_remote_copy(
        src_ref=full.at[:, pl.ds(rows, margin)],
        dst_ref=full.at[:, pl.ds(0, margin)],
        send_sem=sent_edge.at[0],
        recv_sem=got_edge.at[0],
        device_id={"sky": lax.rem(sky + 1, patches)},
        device_id_type=MESH,
    )
    down = pltpu.make_async_remote_copy(
        src_ref=full.at[:, pl.ds(margin, margin)],
        dst_ref=full.at[:, pl.ds(rows + margin, margin)],
        send_sem=sent_edge.at[1],
        recv_sem=got_edge.at[1],
        device_id={"sky": lax.rem(sky + patches - 1, patches)},
        device_id_type=MESH,
    )

    @pl.when(has_high)
    def _():
        up.start()

    @pl.when(has_low)
    def _():
        down.start()

    side = lanes // 2
    out_ref[:, :side] = jnp.zeros((rows + 2 * margin, side), out_ref.dtype)
    out_ref[:, side + tiles * lanes :] = jnp.zeros((rows + 2 * margin, side), out_ref.dtype)

    def lay(row, count):
        image = jnp.concatenate([full[t, row : row + count] for t in range(tiles)], axis=1)
        out_ref[row : row + count, side : side + tiles * lanes] = image.astype(out_ref.dtype)

    lay(margin, rows)

    @pl.when(has_low)
    def _():
        up.wait_recv()

    @pl.when(has_high)
    def _():
        down.wait_recv()

    lay(0, margin)
    lay(rows + margin, margin)

    @pl.when(has_high)
    def _():
        up.wait_send()

    @pl.when(has_low)
    def _():
        down.wait_send()

    for copy in shares:
        copy.wait_send()


def padded_coadd(sizes, margin, partial_sums, partial_high, partial_low, tallies):
    tiles, rows, lanes = partial_sums.shape
    n = sizes[0] * sizes[1]
    return pl.pallas_call(
        functools.partial(coadd_kernel, sizes, margin),
        out_shape=jax.ShapeDtypeStruct((rows + 2 * margin, (tiles + 1) * lanes), jnp.float32),
        in_specs=[pl.BlockSpec(memory_space=pltpu.VMEM)] * 4,
        out_specs=pl.BlockSpec(memory_space=pltpu.VMEM),
        scratch_shapes=[
            pltpu.VMEM((n - 1, 3, tiles, rows // n, lanes), jnp.bfloat16),
            pltpu.VMEM((tiles, rows + 2 * margin, lanes), jnp.bfloat16),
            pltpu.SemaphoreType.DMA((n - 1, 3)),
            pltpu.SemaphoreType.DMA((n - 1, 3)),
            pltpu.SemaphoreType.DMA((n - 1,)),
            pltpu.SemaphoreType.DMA((n - 1,)),
            pltpu.SemaphoreType.DMA((2,)),
            pltpu.SemaphoreType.DMA((2,)),
        ],
        compiler_params=pltpu.CompilerParams(
            collective_id=1, has_side_effects=True, vmem_limit_bytes=24 * 2**20
        ),
    )(partial_sums, partial_high, partial_low, tallies)


def difference_kernel(basis_count, kernel_side, mix_ref, pad_ref, row_ref, slab_ref, valid_ref, out_ref, acc):
    visit_count, tiles, side, _ = slab_ref.shape
    source = lax.broadcasted_iota(jnp.int32, (side, side), 0)
    target = lax.broadcasted_iota(jnp.int32, (side, side), 1)
    first, second = source > target, source < target

    def product(dy):
        upper, lower = [], []
        for b in range(basis_count):
            row = row_ref[pl.ds(dy * basis_count + b, 1), :]
            ring = pltpu.roll(
                jnp.broadcast_to(row, (side, side)), 0, axis=1, stride=1, stride_axis=0
            )
            upper.append(jnp.where(first, ring, 0.0).astype(jnp.bfloat16))
            lower.append(jnp.where(second, ring, 0.0).astype(jnp.bfloat16))
        band = jnp.concatenate(
            [jnp.concatenate(upper, axis=1), jnp.concatenate(lower, axis=1)], axis=0
        )
        height = pad_ref.shape[0]
        turned = pltpu.roll(pad_ref[...], lax.rem(height - dy, height), axis=0)
        shifted = turned[:side].astype(jnp.bfloat16)
        windows = jnp.concatenate(
            [shifted[:, t * side : (t + 2) * side] for t in range(tiles)], axis=0
        )
        return jnp.dot(windows, band, preferred_element_type=jnp.float32)

    acc[...] = product(0)

    def step(i, carry):
        acc[...] += product(2 * i + 1) + product(2 * i + 2)
        return carry

    lax.fori_loop(0, (kernel_side - 1) // 2, step, 0)

    for t in range(tiles):
        planes = [
            acc[t * side : (t + 1) * side, b * side : (b + 1) * side]
            .astype(jnp.bfloat16)
            .astype(jnp.float32)
            for b in range(basis_count)
        ]
        for v in range(visit_count):
            template = mix_ref[v, t * basis_count] * planes[0]
            for b in range(1, basis_count):
                template += mix_ref[v, t * basis_count + b] * planes[b]
            out_ref[v, :, t * side : (t + 1) * side] = (
                (slab_ref[v, t].astype(jnp.float32) - template)
                * valid_ref[v, t].astype(jnp.float32)
            ).astype(out_ref.dtype)


def filter_and_subtract(mixture, padded, kernels, slab_tiles, valid):
    visit_count, tiles, side, _ = slab_tiles.shape
    basis_count, kernel_side = kernels.shape[:2]
    margin = kernel_side // 2
    rows = jnp.pad(kernels.astype(jnp.float32), ((0, 0), (0, 0), (0, side - kernel_side)))
    rows = jnp.roll(jnp.flip(rows, axis=2), -(side // 2 - margin - 1), axis=2)
    rows = jnp.transpose(rows, (1, 0, 2)).reshape(kernel_side * basis_count, side)
    vmem = pl.BlockSpec(memory_space=pltpu.VMEM)
    return pl.pallas_call(
        functools.partial(difference_kernel, basis_count, kernel_side),
        out_shape=jax.ShapeDtypeStruct((visit_count, side, tiles * side), jnp.bfloat16),
        in_specs=[pl.BlockSpec(memory_space=pltpu.SMEM), vmem, vmem, vmem, vmem],
        out_specs=vmem,
        scratch_shapes=[pltpu.VMEM((tiles * side, basis_count * side), jnp.float32)],
        compiler_params=pltpu.CompilerParams(vmem_limit_bytes=48 * 2**20),
    )(mixture.reshape(visit_count, tiles * basis_count), padded, rows, slab_tiles, valid)


def on_device(
    raw_tiles,
    pixel_offsets,
    shift_entry_index,
    shift_table,
    tile_routes,
    bad_pixels,
    basis_kernels,
    basis_choice,
    coef_table,
):
    visit_count, tile_cols, tile_side = (raw_tiles.shape[0], raw_tiles.shape[1], raw_tiles.shape[2])
    tile_area = tile_side * tile_side
    patches = lax.axis_size("sky")
    capacity = (visit_count * tile_cols + patches - 1) // patches + 1
    seat_count = patches * capacity
    warped = warp_tiles(raw_tiles, pixel_offsets, shift_entry_index, shift_table)
    owners = tile_routes // tile_cols
    slot_ids = tile_routes % tile_cols
    before = jnp.arange(tile_cols)[None, :] < jnp.arange(tile_cols)[:, None]
    shared = owners[:, None, :] == owners[:, :, None]
    queue_rank = jnp.sum(shared & before[None], axis=2)
    seat_ids = owners * capacity + queue_rank
    layout = seat_ids[:, None, :] == jnp.arange(seat_count)[None, :, None]
    outgoing = jnp.einsum(
        "vsk,vkx->vsx",
        layout.astype(jnp.bfloat16),
        warped.reshape(visit_count, tile_cols, tile_area),
        preferred_element_type=jnp.float32,
    ).astype(jnp.bfloat16)
    labels = (jnp.sum(jnp.where(layout, slot_ids[:, None, :] + 1, 0), axis=2) - 1).astype(
        jnp.bfloat16
    )
    arrived, arrived_labels = (
        lax.all_to_all(
            outgoing.reshape(visit_count, patches, capacity * tile_area),
            "sky",
            split_axis=1,
            concat_axis=1,
            tiled=True,
        ),
        lax.all_to_all(
            labels.reshape(visit_count, patches, capacity),
            "sky",
            split_axis=1,
            concat_axis=1,
            tiled=True,
        ),
    )
    landing = (
        arrived_labels.astype(jnp.float32).reshape(visit_count, seat_count)[:, None, :]
        == jnp.arange(tile_cols).astype(jnp.float32)[None, :, None]
    )
    placed = jnp.einsum(
        "vks,vsx->vkx",
        landing.astype(jnp.bfloat16),
        arrived.reshape(visit_count, seat_count, tile_area),
        preferred_element_type=jnp.float32,
    ).astype(jnp.bfloat16)
    slab_tiles = placed.reshape(visit_count, tile_cols, tile_side, tile_side)
    sizes = tuple(lax.axis_size(axis) for axis in ("visit", "band", "sky"))
    shard_index = lax.axis_index(("visit", "band"))
    visit_total = bad_pixels.shape[0]
    listed_count = bad_pixels.shape[2]
    own_listed = lax.dynamic_slice_in_dim(bad_pixels, shard_index * visit_count, visit_count, 0)
    valid_pixel_mask = 1.0 - hit_planes(own_listed, tile_side)
    all_listed = jnp.transpose(bad_pixels, (1, 0, 2)).reshape(
        tile_cols, visit_total * listed_count
    )
    tallies = (visit_total - hit_planes(all_listed, tile_side)).astype(jnp.bfloat16)
    values = slab_tiles.astype(jnp.float32)
    partial_sums = jnp.sum(valid_pixel_mask * values, axis=0).astype(jnp.bfloat16)
    partial_high = jnp.max(jnp.where(valid_pixel_mask > 0.5, slab_tiles, -jnp.inf), axis=0)
    partial_low = jnp.min(jnp.where(valid_pixel_mask > 0.5, slab_tiles, jnp.inf), axis=0)
    margin = basis_kernels.shape[-1] // 2
    padded = padded_coadd(sizes, margin, partial_sums, partial_high, partial_low, tallies)
    entries = coef_table.shape[0]
    picks = (basis_choice[..., None] == jnp.arange(entries)).astype(jnp.float32)
    mixture = jnp.sum(picks[..., None] * coef_table, axis=2)
    return filter_and_subtract(
        mixture, padded, basis_kernels, slab_tiles, valid_pixel_mask.astype(jnp.bfloat16)
    )


def solution(mesh):
    return jax.shard_map(
        on_device,
        mesh=mesh,
        in_specs=(
            P(("group", "visit", "band"), "sky", None, None),
            P(("group", "visit", "band"), "sky", None),
            P(("group", "visit", "band"), "sky"),
            P(),
            P(("group", "visit", "band"), "sky"),
            P("group", "sky", None),
            P(),
            P(("group", "visit", "band"), "sky"),
            P(),
        ),
        out_specs=P(("group", "visit", "band"), "sky", None),
        check_vma=False,
    )
```

```python
import functools

import jax
import jax.numpy as jnp
from jax import lax
from jax.experimental import pallas as pl
from jax.experimental.pallas import tpu as pltpu
from jax.sharding import PartitionSpec as P


def lanczos(offset):
    return jnp.where(jnp.abs(offset) < 3.0, jnp.sinc(offset) * jnp.sinc(offset / 3.0), 0.0)


def hit_planes(listed, tile_side):
    indices = jnp.arange(tile_side)
    row_match_count = (listed[..., None, :] // tile_side == indices[:, None]).astype(jnp.bfloat16)
    column_match_count = (listed[..., None, :] % tile_side == indices[:, None]).astype(jnp.bfloat16)
    return jnp.einsum(
        "...am,...bm->...ab",
        row_match_count,
        column_match_count,
        preferred_element_type=jnp.float32,
    )


def warp_tiles(raw_tiles, pixel_offsets, shift_entry_index, shift_table):
    entries = shift_table.shape[0]
    tile_side = raw_tiles.shape[-1]
    selected_entries = (shift_entry_index[..., None] == jnp.arange(entries)).astype(jnp.float32)
    fraction = jnp.sum(selected_entries[..., None] * shift_table, axis=-2)
    shifts = pixel_offsets.astype(jnp.float32) + fraction
    target_positions = jnp.arange(tile_side).astype(jnp.float32)
    spacing = target_positions[:, None] - target_positions[None, :]
    row_weights = lanczos(spacing - shifts[..., 0, None, None]).astype(jnp.bfloat16)
    col_weights = lanczos(spacing - shifts[..., 1, None, None]).astype(jnp.bfloat16)
    halfway = jnp.einsum(
        "vtap,vtpq->vtaq", row_weights, raw_tiles, preferred_element_type=jnp.float32
    ).astype(jnp.bfloat16)
    return jnp.einsum(
        "vtaq,vtbq->vtab", halfway, col_weights, preferred_element_type=jnp.float32
    ).astype(jnp.bfloat16)


MESH = pl.DeviceIdType.MESH


def coadd_kernel(
    sizes, margin, sum_ref, high_ref, low_ref, tally_ref, out_ref,
    got, full, sent_parts, got_parts, sent_rows, got_rows, sent_edge, got_edge,
):
    visits, bands, patches = sizes
    n = visits * bands
    tiles, rows, lanes = sum_ref.shape
    chunk = rows // n
    me = lax.axis_index("visit") * bands + lax.axis_index("band")
    sky = lax.axis_index("sky")
    has_low, has_high = sky > 0, sky < patches - 1

    def place(k):
        peer = lax.rem(me + k, n)
        return peer, {"visit": peer // bands, "band": lax.rem(peer, bands)}

    barrier = pltpu.get_barrier_semaphore()
    for k in range(1, n):
        pl.semaphore_signal(barrier, inc=1, device_id=place(k)[1], device_id_type=MESH)

    @pl.when(has_low)
    def _():
        pl.semaphore_signal(barrier, inc=1, device_id={"sky": sky - 1}, device_id_type=MESH)

    @pl.when(has_high)
    def _():
        pl.semaphore_signal(barrier, inc=1, device_id={"sky": sky + 1}, device_id_type=MESH)

    neighbours = (sky + patches - 1) // patches + (2 * patches - 2 - sky) // patches
    pl.semaphore_wait(barrier, n - 1 + neighbours)

    parts = (sum_ref, high_ref, low_ref)
    copies = []
    for k in range(1, n):
        peer, where = place(k)
        peer_rows = pl.ds(pl.multiple_of(peer * chunk, chunk), chunk)
        for i, part in enumerate(parts):
            copy = pltpu.make_async_remote_copy(
                src_ref=part.at[:, peer_rows],
                dst_ref=got.at[k - 1, i],
                send_sem=sent_parts.at[k - 1, i],
                recv_sem=got_parts.at[k - 1, i],
                device_id=where,
                device_id_type=MESH,
            )
            copy.start()
            copies.append(copy)

    @pl.when(jnp.logical_not(has_low))
    def _():
        full[:, :margin] = jnp.zeros((tiles, margin, lanes), full.dtype)

    @pl.when(jnp.logical_not(has_high))
    def _():
        full[:, rows + margin :] = jnp.zeros((tiles, margin, lanes), full.dtype)

    own_rows = pl.ds(pl.multiple_of(me * chunk, chunk), chunk)
    total, high, low = (part[:, own_rows].astype(jnp.float32) for part in parts)
    for copy in copies:
        copy.wait_recv()
    for k in range(n - 1):
        total += got[k, 0].astype(jnp.float32)
        high = jnp.maximum(high, got[k, 1].astype(jnp.float32))
        low = jnp.minimum(low, got[k, 2].astype(jnp.float32))
    count = tally_ref[:, own_rows].astype(jnp.float32)
    full_rows = pl.ds(pl.multiple_of(margin + me * chunk, 16), chunk)
    full[:, full_rows] = ((total - high - low) / (count - 2.0)).astype(full.dtype)

    shares = []
    for k in range(1, n):
        copy = pltpu.make_async_remote_copy(
            src_ref=full.at[:, full_rows],
            dst_ref=full.at[:, full_rows],
            send_sem=sent_rows.at[k - 1],
            recv_sem=got_rows.at[k - 1],
            device_id=place(k)[1],
            device_id_type=MESH,
        )
        copy.start()
        shares.append(copy)
    for copy in copies:
        copy.wait_send()
    for copy in shares:
        copy.wait_recv()

    up = pltpu.make_async_remote_copy(
        src_ref=full.at[:, pl.ds(rows, margin)],
        dst_ref=full.at[:, pl.ds(0, margin)],
        send_sem=sent_edge.at[0],
        recv_sem=got_edge.at[0],
        device_id={"sky": lax.rem(sky + 1, patches)},
        device_id_type=MESH,
    )
    down = pltpu.make_async_remote_copy(
        src_ref=full.at[:, pl.ds(margin, margin)],
        dst_ref=full.at[:, pl.ds(rows + margin, margin)],
        send_sem=sent_edge.at[1],
        recv_sem=got_edge.at[1],
        device_id={"sky": lax.rem(sky + patches - 1, patches)},
        device_id_type=MESH,
    )

    @pl.when(has_high)
    def _():
        up.start()

    @pl.when(has_low)
    def _():
        down.start()

    side = lanes // 2
    out_ref[:, :side] = jnp.zeros((rows + 2 * margin, side), out_ref.dtype)
    out_ref[:, side + tiles * lanes :] = jnp.zeros((rows + 2 * margin, side), out_ref.dtype)

    def lay(row, count):
        image = jnp.concatenate([full[t, row : row + count] for t in range(tiles)], axis=1)
        out_ref[row : row + count, side : side + tiles * lanes] = image.astype(out_ref.dtype)

    lay(margin, rows)

    @pl.when(has_low)
    def _():
        up.wait_recv()

    @pl.when(has_high)
    def _():
        down.wait_recv()

    lay(0, margin)
    lay(rows + margin, margin)

    @pl.when(has_high)
    def _():
        up.wait_send()

    @pl.when(has_low)
    def _():
        down.wait_send()

    for copy in shares:
        copy.wait_send()


def padded_coadd(sizes, margin, partial_sums, partial_high, partial_low, tallies):
    tiles, rows, lanes = partial_sums.shape
    n = sizes[0] * sizes[1]
    return pl.pallas_call(
        functools.partial(coadd_kernel, sizes, margin),
        out_shape=jax.ShapeDtypeStruct((rows + 2 * margin, (tiles + 1) * lanes), jnp.float32),
        in_specs=[pl.BlockSpec(memory_space=pltpu.VMEM)] * 4,
        out_specs=pl.BlockSpec(memory_space=pltpu.VMEM),
        scratch_shapes=[
            pltpu.VMEM((n - 1, 3, tiles, rows // n, lanes), jnp.bfloat16),
            pltpu.VMEM((tiles, rows + 2 * margin, lanes), jnp.bfloat16),
            pltpu.SemaphoreType.DMA((n - 1, 3)),
            pltpu.SemaphoreType.DMA((n - 1, 3)),
            pltpu.SemaphoreType.DMA((n - 1,)),
            pltpu.SemaphoreType.DMA((n - 1,)),
            pltpu.SemaphoreType.DMA((2,)),
            pltpu.SemaphoreType.DMA((2,)),
        ],
        compiler_params=pltpu.CompilerParams(
            collective_id=1, has_side_effects=True, vmem_limit_bytes=24 * 2**20
        ),
    )(partial_sums, partial_high, partial_low, tallies)


def exchange_kernel(
    source_ref, warped_ref, label_ref, out_ref, out_label_ref,
    stage, landed, landed_labels, sent, received, sent_labels, received_labels,
):
    patches, capacity = stage.shape[:2]
    sky = lax.axis_index("sky")
    barrier = pltpu.get_barrier_semaphore()
    for k in range(1, patches):
        peer = lax.rem(sky + k, patches)
        pl.semaphore_signal(barrier, inc=1, device_id={"sky": peer}, device_id_type=MESH)
    for k in range(patches):
        block = lax.rem(sky + k, patches)
        for c in range(capacity):
            stage[k, c] = warped_ref[source_ref[block * capacity + c]]
    pl.semaphore_wait(barrier, patches - 1)
    copies = []
    for k in range(1, patches):
        peer = lax.rem(sky + k, patches)
        for src, dst, gone, come in (
            (stage.at[k], landed.at[k], sent, received),
            (label_ref.at[peer], landed_labels.at[k], sent_labels, received_labels),
        ):
            copy = pltpu.make_async_remote_copy(
                src_ref=src,
                dst_ref=dst,
                send_sem=gone.at[k],
                recv_sem=come.at[k],
                device_id={"sky": peer},
                device_id_type=MESH,
            )
            copy.start()
            copies.append(copy)
    out_ref[0] = stage[0]
    out_label_ref[0] = label_ref[sky]
    for i, copy in enumerate(copies):
        copy.wait_recv()
        k = i // 2 + 1
        if i % 2 == 0:
            out_ref[k] = landed[k]
        else:
            out_label_ref[k] = landed_labels[k]
    for copy in copies:
        copy.wait_send()


def exchange_tiles(sources, warped, labels):
    patches, capacity = labels.shape
    side = warped.shape[-1]
    spread = jnp.pad(
        labels.astype(jnp.bfloat16)[:, None, :], ((0, 0), (0, 15), (0, side - capacity))
    )
    vmem = pl.BlockSpec(memory_space=pltpu.VMEM)
    tiles = (patches, capacity, side, side)
    arrived, arrived_labels = pl.pallas_call(
        exchange_kernel,
        out_shape=(
            jax.ShapeDtypeStruct(tiles, jnp.bfloat16),
            jax.ShapeDtypeStruct(spread.shape, jnp.bfloat16),
        ),
        in_specs=[pl.BlockSpec(memory_space=pltpu.SMEM), vmem, vmem],
        out_specs=(vmem, vmem),
        scratch_shapes=[
            pltpu.VMEM(tiles, jnp.bfloat16),
            pltpu.VMEM(tiles, jnp.bfloat16),
            pltpu.VMEM(spread.shape, jnp.bfloat16),
            pltpu.SemaphoreType.DMA((patches,)),
            pltpu.SemaphoreType.DMA((patches,)),
            pltpu.SemaphoreType.DMA((patches,)),
            pltpu.SemaphoreType.DMA((patches,)),
        ],
        compiler_params=pltpu.CompilerParams(
            collective_id=2, has_side_effects=True, vmem_limit_bytes=32 * 2**20
        ),
    )(sources, warped, spread)
    return arrived, arrived_labels[:, 0, :capacity]


def place_kernel(seat_ref, arrived_ref, valid_ref, slab_ref, sum_ref, high_ref, low_ref):
    visit_count, tiles = slab_ref.shape[:2]

    def step(t, carry):
        total = high = low = None
        for v in range(visit_count):
            tile = arrived_ref[seat_ref[v * tiles + t]]
            slab_ref[v, t] = tile
            value = tile.astype(jnp.float32)
            usable = valid_ref[v, t].astype(jnp.float32)
            at_most = jnp.where(usable > 0.5, value, -jnp.inf)
            at_least = jnp.where(usable > 0.5, value, jnp.inf)
            if total is None:
                total, high, low = usable * value, at_most, at_least
            else:
                total = total + usable * value
                high, low = jnp.maximum(high, at_most), jnp.minimum(low, at_least)
        sum_ref[t] = total.astype(sum_ref.dtype)
        high_ref[t] = high.astype(high_ref.dtype)
        low_ref[t] = low.astype(low_ref.dtype)
        return carry

    lax.fori_loop(0, tiles, step, 0)


def place_tiles(seats, arrived, valid):
    visit_count, tiles, side, _ = valid.shape
    vmem = pl.BlockSpec(memory_space=pltpu.VMEM)
    plane = jax.ShapeDtypeStruct((tiles, side, side), jnp.bfloat16)
    return pl.pallas_call(
        place_kernel,
        out_shape=(jax.ShapeDtypeStruct(valid.shape, jnp.bfloat16), plane, plane, plane),
        in_specs=[pl.BlockSpec(memory_space=pltpu.SMEM), vmem, vmem],
        out_specs=(vmem,) * 4,
        compiler_params=pltpu.CompilerParams(vmem_limit_bytes=24 * 2**20),
    )(seats, arrived, valid)


def difference_kernel(basis_count, kernel_side, mix_ref, pad_ref, row_ref, slab_ref, valid_ref, out_ref, acc):
    visit_count, tiles, side, _ = slab_ref.shape
    source = lax.broadcasted_iota(jnp.int32, (side, side), 0)
    target = lax.broadcasted_iota(jnp.int32, (side, side), 1)
    first, second = source > target, source < target

    def product(dy):
        upper, lower = [], []
        for b in range(basis_count):
            row = row_ref[pl.ds(dy * basis_count + b, 1), :]
            ring = pltpu.roll(
                jnp.broadcast_to(row, (side, side)), 0, axis=1, stride=1, stride_axis=0
            )
            upper.append(jnp.where(first, ring, 0.0).astype(jnp.bfloat16))
            lower.append(jnp.where(second, ring, 0.0).astype(jnp.bfloat16))
        band = jnp.concatenate(
            [jnp.concatenate(upper, axis=1), jnp.concatenate(lower, axis=1)], axis=0
        )
        height = pad_ref.shape[0]
        turned = pltpu.roll(pad_ref[...], lax.rem(height - dy, height), axis=0)
        shifted = turned[:side].astype(jnp.bfloat16)
        windows = jnp.concatenate(
            [shifted[:, t * side : (t + 2) * side] for t in range(tiles)], axis=0
        )
        return jnp.dot(windows, band, preferred_element_type=jnp.float32)

    acc[...] = product(0)

    def step(i, carry):
        acc[...] += product(2 * i + 1) + product(2 * i + 2)
        return carry

    lax.fori_loop(0, (kernel_side - 1) // 2, step, 0)

    for t in range(tiles):
        planes = [
            acc[t * side : (t + 1) * side, b * side : (b + 1) * side]
            .astype(jnp.bfloat16)
            .astype(jnp.float32)
            for b in range(basis_count)
        ]
        for v in range(visit_count):
            template = mix_ref[v, t * basis_count] * planes[0]
            for b in range(1, basis_count):
                template += mix_ref[v, t * basis_count + b] * planes[b]
            out_ref[v, :, t * side : (t + 1) * side] = (
                (slab_ref[v, t].astype(jnp.float32) - template)
                * valid_ref[v, t].astype(jnp.float32)
            ).astype(out_ref.dtype)


def filter_and_subtract(mixture, padded, kernels, slab_tiles, valid):
    visit_count, tiles, side, _ = slab_tiles.shape
    basis_count, kernel_side = kernels.shape[:2]
    margin = kernel_side // 2
    rows = jnp.pad(kernels.astype(jnp.float32), ((0, 0), (0, 0), (0, side - kernel_side)))
    rows = jnp.roll(jnp.flip(rows, axis=2), -(side // 2 - margin - 1), axis=2)
    rows = jnp.transpose(rows, (1, 0, 2)).reshape(kernel_side * basis_count, side)
    vmem = pl.BlockSpec(memory_space=pltpu.VMEM)
    return pl.pallas_call(
        functools.partial(difference_kernel, basis_count, kernel_side),
        out_shape=jax.ShapeDtypeStruct((visit_count, side, tiles * side), jnp.bfloat16),
        in_specs=[pl.BlockSpec(memory_space=pltpu.SMEM), vmem, vmem, vmem, vmem],
        out_specs=vmem,
        scratch_shapes=[pltpu.VMEM((tiles * side, basis_count * side), jnp.float32)],
        compiler_params=pltpu.CompilerParams(vmem_limit_bytes=48 * 2**20),
    )(mixture.reshape(visit_count, tiles * basis_count), padded, rows, slab_tiles, valid)


def on_device(
    raw_tiles,
    pixel_offsets,
    shift_entry_index,
    shift_table,
    tile_routes,
    bad_pixels,
    basis_kernels,
    basis_choice,
    coef_table,
):
    visit_count, tile_cols, tile_side = (raw_tiles.shape[0], raw_tiles.shape[1], raw_tiles.shape[2])
    patches = lax.axis_size("sky")
    pooled = visit_count * tile_cols
    capacity = (pooled + patches - 1) // patches + 1
    owners = (tile_routes // tile_cols).reshape(pooled)
    slots = (tile_routes % tile_cols + tile_cols * jnp.arange(visit_count)[:, None]).reshape(pooled)
    order = jnp.arange(pooled)
    earlier = (owners[None, :] == owners[:, None]) & (order[None, :] < order[:, None])
    seat_ids = owners * capacity + jnp.sum(earlier, axis=1)
    layout = seat_ids[None, :] == jnp.arange(patches * capacity)[:, None]
    sources = jnp.sum(jnp.where(layout, order[None, :], 0), axis=1)
    labels = jnp.sum(jnp.where(layout, slots[None, :] + 1, 0), axis=1) - 1
    warped = warp_tiles(raw_tiles, pixel_offsets, shift_entry_index, shift_table)
    arrived, arrived_labels = exchange_tiles(
        sources,
        warped.reshape(pooled, tile_side, tile_side),
        labels.reshape(patches, capacity),
    )
    landing = arrived_labels.astype(jnp.float32).reshape(1, -1) == order.astype(jnp.float32)[:, None]
    seats = jnp.sum(jnp.where(landing, jnp.arange(patches * capacity)[None, :], 0), axis=1)
    sizes = tuple(lax.axis_size(axis) for axis in ("visit", "band", "sky"))
    shard_index = lax.axis_index(("visit", "band"))
    visit_total = bad_pixels.shape[0]
    listed_count = bad_pixels.shape[2]
    own_listed = lax.dynamic_slice_in_dim(bad_pixels, shard_index * visit_count, visit_count, 0)
    valid_pixel_mask = 1.0 - hit_planes(own_listed, tile_side)
    all_listed = jnp.transpose(bad_pixels, (1, 0, 2)).reshape(
        tile_cols, visit_total * listed_count
    )
    tallies = (visit_total - hit_planes(all_listed, tile_side)).astype(jnp.bfloat16)
    valid = valid_pixel_mask.astype(jnp.bfloat16)
    slab_tiles, partial_sums, partial_high, partial_low = place_tiles(
        seats, arrived.reshape(patches * capacity, tile_side, tile_side), valid
    )
    margin = basis_kernels.shape[-1] // 2
    padded = padded_coadd(sizes, margin, partial_sums, partial_high, partial_low, tallies)
    entries = coef_table.shape[0]
    picks = (basis_choice[..., None] == jnp.arange(entries)).astype(jnp.float32)
    mixture = jnp.sum(picks[..., None] * coef_table, axis=2)
    return filter_and_subtract(
        mixture, padded, basis_kernels, slab_tiles, valid
    )


def solution(mesh):
    return jax.shard_map(
        on_device,
        mesh=mesh,
        in_specs=(
            P(("group", "visit", "band"), "sky", None, None),
            P(("group", "visit", "band"), "sky", None),
            P(("group", "visit", "band"), "sky"),
            P(),
            P(("group", "visit", "band"), "sky"),
            P("group", "sky", None),
            P(),
            P(("group", "visit", "band"), "sky"),
            P(),
        ),
        out_specs=P(("group", "visit", "band"), "sky", None),
        check_vma=False,
    )
```

```python
import functools

import jax
import jax.numpy as jnp
from jax import lax
from jax.experimental import pallas as pl
from jax.experimental.pallas import tpu as pltpu
from jax.sharding import PartitionSpec as P


def lanczos(offset):
    return jnp.where(jnp.abs(offset) < 3.0, jnp.sinc(offset) * jnp.sinc(offset / 3.0), 0.0)


def hit_planes(listed, tile_side):
    indices = jnp.arange(tile_side)
    row_match_count = (listed[..., None, :] // tile_side == indices[:, None]).astype(jnp.bfloat16)
    column_match_count = (listed[..., None, :] % tile_side == indices[:, None]).astype(jnp.bfloat16)
    return jnp.einsum(
        "...am,...bm->...ab",
        row_match_count,
        column_match_count,
        preferred_element_type=jnp.float32,
    )


def warp_tiles(raw_tiles, pixel_offsets, shift_entry_index, shift_table):
    entries = shift_table.shape[0]
    tile_side = raw_tiles.shape[-1]
    selected_entries = (shift_entry_index[..., None] == jnp.arange(entries)).astype(jnp.float32)
    fraction = jnp.sum(selected_entries[..., None] * shift_table, axis=-2)
    shifts = pixel_offsets.astype(jnp.float32) + fraction
    target_positions = jnp.arange(tile_side).astype(jnp.float32)
    spacing = target_positions[:, None] - target_positions[None, :]
    row_weights = lanczos(spacing - shifts[..., 0, None, None]).astype(jnp.bfloat16)
    col_weights = lanczos(spacing - shifts[..., 1, None, None]).astype(jnp.bfloat16)
    halfway = jnp.einsum(
        "vtap,vtpq->vtaq", row_weights, raw_tiles, preferred_element_type=jnp.float32
    ).astype(jnp.bfloat16)
    return jnp.einsum(
        "vtaq,vtbq->vtab", halfway, col_weights, preferred_element_type=jnp.float32
    ).astype(jnp.bfloat16)


MESH = pl.DeviceIdType.MESH


def coadd_kernel(
    sizes, margin, sum_ref, high_ref, low_ref, tally_ref, out_ref,
    got, full, sent_parts, got_parts, sent_rows, got_rows, sent_edge, got_edge,
):
    visits, bands, patches = sizes
    n = visits * bands
    tiles, rows, lanes = sum_ref.shape
    chunk = rows // n
    me = lax.axis_index("visit") * bands + lax.axis_index("band")
    sky = lax.axis_index("sky")
    has_low, has_high = sky > 0, sky < patches - 1

    def place(k):
        peer = lax.rem(me + k, n)
        return peer, {"visit": peer // bands, "band": lax.rem(peer, bands)}

    barrier = pltpu.get_barrier_semaphore()
    for k in range(1, n):
        pl.semaphore_signal(barrier, inc=1, device_id=place(k)[1], device_id_type=MESH)

    @pl.when(has_low)
    def _():
        pl.semaphore_signal(barrier, inc=1, device_id={"sky": sky - 1}, device_id_type=MESH)

    @pl.when(has_high)
    def _():
        pl.semaphore_signal(barrier, inc=1, device_id={"sky": sky + 1}, device_id_type=MESH)

    neighbours = (sky + patches - 1) // patches + (2 * patches - 2 - sky) // patches
    pl.semaphore_wait(barrier, n - 1 + neighbours)

    parts = (sum_ref, high_ref, low_ref)
    copies = []
    for k in range(1, n):
        peer, where = place(k)
        peer_rows = pl.ds(pl.multiple_of(peer * chunk, chunk), chunk)
        for i, part in enumerate(parts):
            copy = pltpu.make_async_remote_copy(
                src_ref=part.at[:, peer_rows],
                dst_ref=got.at[k - 1, i],
                send_sem=sent_parts.at[k - 1, i],
                recv_sem=got_parts.at[k - 1, i],
                device_id=where,
                device_id_type=MESH,
            )
            copy.start()
            copies.append(copy)

    @pl.when(jnp.logical_not(has_low))
    def _():
        full[:, :margin] = jnp.zeros((tiles, margin, lanes), full.dtype)

    @pl.when(jnp.logical_not(has_high))
    def _():
        full[:, rows + margin :] = jnp.zeros((tiles, margin, lanes), full.dtype)

    own_rows = pl.ds(pl.multiple_of(me * chunk, chunk), chunk)
    total, high, low = (part[:, own_rows].astype(jnp.float32) for part in parts)
    for copy in copies:
        copy.wait_recv()
    for k in range(n - 1):
        total += got[k, 0].astype(jnp.float32)
        high = jnp.maximum(high, got[k, 1].astype(jnp.float32))
        low = jnp.minimum(low, got[k, 2].astype(jnp.float32))
    count = tally_ref[:, own_rows].astype(jnp.float32)
    full_rows = pl.ds(pl.multiple_of(margin + me * chunk, 16), chunk)
    full[:, full_rows] = ((total - high - low) / (count - 2.0)).astype(full.dtype)

    shares = []
    for k in range(1, n):
        copy = pltpu.make_async_remote_copy(
            src_ref=full.at[:, full_rows],
            dst_ref=full.at[:, full_rows],
            send_sem=sent_rows.at[k - 1],
            recv_sem=got_rows.at[k - 1],
            device_id=place(k)[1],
            device_id_type=MESH,
        )
        copy.start()
        shares.append(copy)
    for copy in copies:
        copy.wait_send()
    for copy in shares:
        copy.wait_recv()

    up = pltpu.make_async_remote_copy(
        src_ref=full.at[:, pl.ds(rows, margin)],
        dst_ref=full.at[:, pl.ds(0, margin)],
        send_sem=sent_edge.at[0],
        recv_sem=got_edge.at[0],
        device_id={"sky": lax.rem(sky + 1, patches)},
        device_id_type=MESH,
    )
    down = pltpu.make_async_remote_copy(
        src_ref=full.at[:, pl.ds(margin, margin)],
        dst_ref=full.at[:, pl.ds(rows + margin, margin)],
        send_sem=sent_edge.at[1],
        recv_sem=got_edge.at[1],
        device_id={"sky": lax.rem(sky + patches - 1, patches)},
        device_id_type=MESH,
    )

    @pl.when(has_high)
    def _():
        up.start()

    @pl.when(has_low)
    def _():
        down.start()

    side = lanes // 2
    out_ref[:, :side] = jnp.zeros((rows + 2 * margin, side), out_ref.dtype)
    out_ref[:, side + tiles * lanes :] = jnp.zeros((rows + 2 * margin, side), out_ref.dtype)

    def lay(row, count):
        image = jnp.concatenate([full[t, row : row + count] for t in range(tiles)], axis=1)
        out_ref[row : row + count, side : side + tiles * lanes] = image.astype(out_ref.dtype)

    lay(margin, rows)

    @pl.when(has_low)
    def _():
        up.wait_recv()

    @pl.when(has_high)
    def _():
        down.wait_recv()

    lay(0, margin)
    lay(rows + margin, margin)

    @pl.when(has_high)
    def _():
        up.wait_send()

    @pl.when(has_low)
    def _():
        down.wait_send()

    for copy in shares:
        copy.wait_send()


def padded_coadd(sizes, margin, partial_sums, partial_high, partial_low, tallies):
    tiles, rows, lanes = partial_sums.shape
    n = sizes[0] * sizes[1]
    return pl.pallas_call(
        functools.partial(coadd_kernel, sizes, margin),
        out_shape=jax.ShapeDtypeStruct((rows + 2 * margin, (tiles + 1) * lanes), jnp.float32),
        in_specs=[pl.BlockSpec(memory_space=pltpu.VMEM)] * 4,
        out_specs=pl.BlockSpec(memory_space=pltpu.VMEM),
        scratch_shapes=[
            pltpu.VMEM((n - 1, 3, tiles, rows // n, lanes), jnp.bfloat16),
            pltpu.VMEM((tiles, rows + 2 * margin, lanes), jnp.bfloat16),
            pltpu.SemaphoreType.DMA((n - 1, 3)),
            pltpu.SemaphoreType.DMA((n - 1, 3)),
            pltpu.SemaphoreType.DMA((n - 1,)),
            pltpu.SemaphoreType.DMA((n - 1,)),
            pltpu.SemaphoreType.DMA((2,)),
            pltpu.SemaphoreType.DMA((2,)),
        ],
        compiler_params=pltpu.CompilerParams(
            collective_id=1, has_side_effects=True, vmem_limit_bytes=24 * 2**20
        ),
    )(partial_sums, partial_high, partial_low, tallies)


def exchange_kernel(
    source_ref, warped_ref, label_ref, out_ref, out_label_ref,
    stage, landed, landed_labels, sent, received, sent_labels, received_labels,
):
    patches, capacity = stage.shape[:2]
    sky = lax.axis_index("sky")
    barrier = pltpu.get_barrier_semaphore()
    for k in range(1, patches):
        peer = lax.rem(sky + k, patches)
        pl.semaphore_signal(barrier, inc=1, device_id={"sky": peer}, device_id_type=MESH)
    for k in range(patches):
        block = lax.rem(sky + k, patches)
        for c in range(capacity):
            stage[k, c] = warped_ref[source_ref[block * capacity + c]]
    pl.semaphore_wait(barrier, patches - 1)
    copies = []
    for k in range(1, patches):
        peer = lax.rem(sky + k, patches)
        for src, dst, gone, come in (
            (stage.at[k], landed.at[k], sent, received),
            (label_ref.at[peer], landed_labels.at[k], sent_labels, received_labels),
        ):
            copy = pltpu.make_async_remote_copy(
                src_ref=src,
                dst_ref=dst,
                send_sem=gone.at[k],
                recv_sem=come.at[k],
                device_id={"sky": peer},
                device_id_type=MESH,
            )
            copy.start()
            copies.append(copy)
    out_ref[0] = stage[0]
    out_label_ref[0] = label_ref[sky]
    for i, copy in enumerate(copies):
        copy.wait_recv()
        k = i // 2 + 1
        if i % 2 == 0:
            out_ref[k] = landed[k]
        else:
            out_label_ref[k] = landed_labels[k]
    for copy in copies:
        copy.wait_send()


def exchange_tiles(sources, warped, labels):
    patches, capacity = labels.shape
    side = warped.shape[-1]
    spread = jnp.pad(
        labels.astype(jnp.bfloat16)[:, None, :], ((0, 0), (0, 15), (0, side - capacity))
    )
    vmem = pl.BlockSpec(memory_space=pltpu.VMEM)
    tiles = (patches, capacity, side, side)
    arrived, arrived_labels = pl.pallas_call(
        exchange_kernel,
        out_shape=(
            jax.ShapeDtypeStruct(tiles, jnp.bfloat16),
            jax.ShapeDtypeStruct(spread.shape, jnp.bfloat16),
        ),
        in_specs=[pl.BlockSpec(memory_space=pltpu.SMEM), vmem, vmem],
        out_specs=(vmem, vmem),
        scratch_shapes=[
            pltpu.VMEM(tiles, jnp.bfloat16),
            pltpu.VMEM(tiles, jnp.bfloat16),
            pltpu.VMEM(spread.shape, jnp.bfloat16),
            pltpu.SemaphoreType.DMA((patches,)),
            pltpu.SemaphoreType.DMA((patches,)),
            pltpu.SemaphoreType.DMA((patches,)),
            pltpu.SemaphoreType.DMA((patches,)),
        ],
        compiler_params=pltpu.CompilerParams(
            collective_id=2, has_side_effects=True, vmem_limit_bytes=32 * 2**20
        ),
    )(sources, warped, spread)
    return arrived, arrived_labels[:, 0, :capacity]


def place_kernel(seat_ref, arrived_ref, valid_ref, slab_ref, sum_ref, high_ref, low_ref):
    visit_count, tiles = slab_ref.shape[:2]

    def step(t, carry):
        total = high = low = None
        for v in range(visit_count):
            tile = arrived_ref[seat_ref[v * tiles + t]]
            slab_ref[v, t] = tile
            value = tile.astype(jnp.float32)
            usable = valid_ref[v, t].astype(jnp.float32)
            at_most = jnp.where(usable > 0.5, value, -jnp.inf)
            at_least = jnp.where(usable > 0.5, value, jnp.inf)
            if total is None:
                total, high, low = usable * value, at_most, at_least
            else:
                total = total + usable * value
                high, low = jnp.maximum(high, at_most), jnp.minimum(low, at_least)
        sum_ref[t] = total.astype(sum_ref.dtype)
        high_ref[t] = high.astype(high_ref.dtype)
        low_ref[t] = low.astype(low_ref.dtype)
        return carry

    lax.fori_loop(0, tiles, step, 0)


def place_tiles(seats, arrived, valid):
    visit_count, tiles, side, _ = valid.shape
    vmem = pl.BlockSpec(memory_space=pltpu.VMEM)
    plane = jax.ShapeDtypeStruct((tiles, side, side), jnp.bfloat16)
    return pl.pallas_call(
        place_kernel,
        out_shape=(jax.ShapeDtypeStruct(valid.shape, jnp.bfloat16), plane, plane, plane),
        in_specs=[pl.BlockSpec(memory_space=pltpu.SMEM), vmem, vmem],
        out_specs=(vmem,) * 4,
        compiler_params=pltpu.CompilerParams(vmem_limit_bytes=24 * 2**20),
    )(seats, arrived, valid)


def difference_kernel(basis_count, kernel_side, mix_ref, pad_ref, row_ref, slab_ref, valid_ref, out_ref, acc, turned):
    visit_count, tiles, side, _ = slab_ref.shape
    source = lax.broadcasted_iota(jnp.int32, (side, side), 0)
    target = lax.broadcasted_iota(jnp.int32, (side, side), 1)
    first, second = source > target, source < target

    def band_of(dy):
        upper, lower = [], []
        for b in range(basis_count):
            row = row_ref[pl.ds(dy * basis_count + b, 1), :]
            ring = pltpu.roll(
                jnp.broadcast_to(row, (side, side)), 0, axis=1, stride=1, stride_axis=0
            )
            upper.append(jnp.where(first, ring, 0.0).astype(jnp.bfloat16))
            lower.append(jnp.where(second, ring, 0.0).astype(jnp.bfloat16))
        return [jnp.concatenate(upper, axis=1), jnp.concatenate(lower, axis=1)]

    def windows_of(ref, r):
        shifted = ref[r : r + side, :].astype(jnp.bfloat16)
        return jnp.concatenate(
            [shifted[:, t * side : (t + 2) * side] for t in range(tiles)], axis=0
        )

    acc[...] = jnp.dot(
        windows_of(pad_ref, 0),
        jnp.concatenate(band_of(0), axis=0),
        preferred_element_type=jnp.float32,
    )
    height = pad_ref.shape[0]
    group = 4 if (kernel_side - 1) % 4 == 0 else 2

    def step(i, carry):
        dy = group * i + 1
        turned[...] = pltpu.roll(pad_ref[...], height - dy, axis=0)
        windows = jnp.concatenate([windows_of(turned, r) for r in range(group)], axis=1)
        band = jnp.concatenate([x for r in range(group) for x in band_of(dy + r)], axis=0)
        acc[...] += jnp.dot(windows, band, preferred_element_type=jnp.float32)
        return carry

    lax.fori_loop(0, (kernel_side - 1) // group, step, 0)

    for t in range(tiles):
        planes = [
            acc[t * side : (t + 1) * side, b * side : (b + 1) * side]
            .astype(jnp.bfloat16)
            .astype(jnp.float32)
            for b in range(basis_count)
        ]
        for v in range(visit_count):
            template = mix_ref[v, t * basis_count] * planes[0]
            for b in range(1, basis_count):
                template += mix_ref[v, t * basis_count + b] * planes[b]
            out_ref[v, :, t * side : (t + 1) * side] = (
                (slab_ref[v, t].astype(jnp.float32) - template)
                * valid_ref[v, t].astype(jnp.float32)
            ).astype(out_ref.dtype)


def filter_and_subtract(mixture, padded, kernels, slab_tiles, valid):
    visit_count, tiles, side, _ = slab_tiles.shape
    basis_count, kernel_side = kernels.shape[:2]
    margin = kernel_side // 2
    rows = jnp.pad(kernels.astype(jnp.float32), ((0, 0), (0, 0), (0, side - kernel_side)))
    rows = jnp.roll(jnp.flip(rows, axis=2), -(side // 2 - margin - 1), axis=2)
    rows = jnp.transpose(rows, (1, 0, 2)).reshape(kernel_side * basis_count, side)
    vmem = pl.BlockSpec(memory_space=pltpu.VMEM)
    return pl.pallas_call(
        functools.partial(difference_kernel, basis_count, kernel_side),
        out_shape=jax.ShapeDtypeStruct((visit_count, side, tiles * side), jnp.bfloat16),
        in_specs=[pl.BlockSpec(memory_space=pltpu.SMEM), vmem, vmem, vmem, vmem],
        out_specs=vmem,
        scratch_shapes=[
            pltpu.VMEM((tiles * side, basis_count * side), jnp.float32),
            pltpu.VMEM(padded.shape, jnp.float32),
        ],
        compiler_params=pltpu.CompilerParams(vmem_limit_bytes=48 * 2**20),
    )(mixture.reshape(visit_count, tiles * basis_count), padded, rows, slab_tiles, valid)


def on_device(
    raw_tiles,
    pixel_offsets,
    shift_entry_index,
    shift_table,
    tile_routes,
    bad_pixels,
    basis_kernels,
    basis_choice,
    coef_table,
):
    visit_count, tile_cols, tile_side = (raw_tiles.shape[0], raw_tiles.shape[1], raw_tiles.shape[2])
    patches = lax.axis_size("sky")
    pooled = visit_count * tile_cols
    capacity = (pooled + patches - 1) // patches + 1
    owners = (tile_routes // tile_cols).reshape(pooled)
    slots = (tile_routes % tile_cols + tile_cols * jnp.arange(visit_count)[:, None]).reshape(pooled)
    order = jnp.arange(pooled)
    earlier = (owners[None, :] == owners[:, None]) & (order[None, :] < order[:, None])
    seat_ids = owners * capacity + jnp.sum(earlier, axis=1)
    layout = seat_ids[None, :] == jnp.arange(patches * capacity)[:, None]
    sources = jnp.sum(jnp.where(layout, order[None, :], 0), axis=1)
    labels = jnp.sum(jnp.where(layout, slots[None, :] + 1, 0), axis=1) - 1
    warped = warp_tiles(raw_tiles, pixel_offsets, shift_entry_index, shift_table)
    arrived, arrived_labels = exchange_tiles(
        sources,
        warped.reshape(pooled, tile_side, tile_side),
        labels.reshape(patches, capacity),
    )
    landing = arrived_labels.astype(jnp.float32).reshape(1, -1) == order.astype(jnp.float32)[:, None]
    seats = jnp.sum(jnp.where(landing, jnp.arange(patches * capacity)[None, :], 0), axis=1)
    sizes = tuple(lax.axis_size(axis) for axis in ("visit", "band", "sky"))
    shard_index = lax.axis_index(("visit", "band"))
    visit_total = bad_pixels.shape[0]
    listed_count = bad_pixels.shape[2]
    own_listed = lax.dynamic_slice_in_dim(bad_pixels, shard_index * visit_count, visit_count, 0)
    valid_pixel_mask = 1.0 - hit_planes(own_listed, tile_side)
    all_listed = jnp.transpose(bad_pixels, (1, 0, 2)).reshape(
        tile_cols, visit_total * listed_count
    )
    tallies = (visit_total - hit_planes(all_listed, tile_side)).astype(jnp.bfloat16)
    valid = valid_pixel_mask.astype(jnp.bfloat16)
    slab_tiles, partial_sums, partial_high, partial_low = place_tiles(
        seats, arrived.reshape(patches * capacity, tile_side, tile_side), valid
    )
    margin = basis_kernels.shape[-1] // 2
    padded = padded_coadd(sizes, margin, partial_sums, partial_high, partial_low, tallies)
    entries = coef_table.shape[0]
    picks = (basis_choice[..., None] == jnp.arange(entries)).astype(jnp.float32)
    mixture = jnp.sum(picks[..., None] * coef_table, axis=2)
    return filter_and_subtract(
        mixture, padded, basis_kernels, slab_tiles, valid
    )


def solution(mesh):
    return jax.shard_map(
        on_device,
        mesh=mesh,
        in_specs=(
            P(("group", "visit", "band"), "sky", None, None),
            P(("group", "visit", "band"), "sky", None),
            P(("group", "visit", "band"), "sky"),
            P(),
            P(("group", "visit", "band"), "sky"),
            P("group", "sky", None),
            P(),
            P(("group", "visit", "band"), "sky"),
            P(),
        ),
        out_specs=P(("group", "visit", "band"), "sky", None),
        check_vma=False,
    )
```

```python
import functools

import jax
import jax.numpy as jnp
from jax import lax
from jax.experimental import pallas as pl
from jax.experimental.pallas import tpu as pltpu
from jax.sharding import PartitionSpec as P


def lanczos(offset):
    return jnp.where(jnp.abs(offset) < 3.0, jnp.sinc(offset) * jnp.sinc(offset / 3.0), 0.0)


def hit_planes(listed, tile_side):
    indices = jnp.arange(tile_side)
    row_match_count = (listed[..., None, :] // tile_side == indices[:, None]).astype(jnp.bfloat16)
    column_match_count = (listed[..., None, :] % tile_side == indices[:, None]).astype(jnp.bfloat16)
    return jnp.einsum(
        "...am,...bm->...ab",
        row_match_count,
        column_match_count,
        preferred_element_type=jnp.float32,
    )


def warp_tiles(raw_tiles, pixel_offsets, shift_entry_index, shift_table):
    entries = shift_table.shape[0]
    tile_side = raw_tiles.shape[-1]
    selected_entries = (shift_entry_index[..., None] == jnp.arange(entries)).astype(jnp.float32)
    fraction = jnp.sum(selected_entries[..., None] * shift_table, axis=-2)
    shifts = pixel_offsets.astype(jnp.float32) + fraction
    target_positions = jnp.arange(tile_side).astype(jnp.float32)
    spacing = target_positions[:, None] - target_positions[None, :]
    row_weights = lanczos(spacing - shifts[..., 0, None, None]).astype(jnp.bfloat16)
    col_weights = lanczos(spacing - shifts[..., 1, None, None]).astype(jnp.bfloat16)
    halfway = jnp.einsum(
        "vtap,vtpq->vtaq", row_weights, raw_tiles, preferred_element_type=jnp.float32
    ).astype(jnp.bfloat16)
    return jnp.einsum(
        "vtaq,vtbq->vtab", halfway, col_weights, preferred_element_type=jnp.float32
    ).astype(jnp.bfloat16)


MESH = pl.DeviceIdType.MESH


def coadd_kernel(
    sizes, margin, sum_ref, high_ref, low_ref, tally_ref, out_ref,
    got, full, sent_parts, got_parts, sent_rows, got_rows, sent_edge, got_edge,
):
    visits, bands, patches = sizes
    n = visits * bands
    tiles, rows, lanes = sum_ref.shape
    chunk = rows // n
    me = lax.axis_index("visit") * bands + lax.axis_index("band")
    sky = lax.axis_index("sky")
    has_low, has_high = sky > 0, sky < patches - 1

    def place(k):
        peer = lax.rem(me + k, n)
        return peer, {"visit": peer // bands, "band": lax.rem(peer, bands)}

    barrier = pltpu.get_barrier_semaphore()
    for k in range(1, n):
        pl.semaphore_signal(barrier, inc=1, device_id=place(k)[1], device_id_type=MESH)

    @pl.when(has_low)
    def _():
        pl.semaphore_signal(barrier, inc=1, device_id={"sky": sky - 1}, device_id_type=MESH)

    @pl.when(has_high)
    def _():
        pl.semaphore_signal(barrier, inc=1, device_id={"sky": sky + 1}, device_id_type=MESH)

    neighbours = (sky + patches - 1) // patches + (2 * patches - 2 - sky) // patches
    pl.semaphore_wait(barrier, n - 1 + neighbours)

    parts = (sum_ref, high_ref, low_ref)
    copies = []
    for k in range(1, n):
        peer, where = place(k)
        peer_rows = pl.ds(pl.multiple_of(peer * chunk, chunk), chunk)
        for i, part in enumerate(parts):
            copy = pltpu.make_async_remote_copy(
                src_ref=part.at[:, peer_rows],
                dst_ref=got.at[k - 1, i],
                send_sem=sent_parts.at[k - 1, i],
                recv_sem=got_parts.at[k - 1, i],
                device_id=where,
                device_id_type=MESH,
            )
            copy.start()
            copies.append(copy)

    @pl.when(jnp.logical_not(has_low))
    def _():
        full[:, :margin] = jnp.zeros((tiles, margin, lanes), full.dtype)

    @pl.when(jnp.logical_not(has_high))
    def _():
        full[:, rows + margin :] = jnp.zeros((tiles, margin, lanes), full.dtype)

    own_rows = pl.ds(pl.multiple_of(me * chunk, chunk), chunk)
    total, high, low = (part[:, own_rows].astype(jnp.float32) for part in parts)
    for copy in copies:
        copy.wait_recv()
    for k in range(n - 1):
        total += got[k, 0].astype(jnp.float32)
        high = jnp.maximum(high, got[k, 1].astype(jnp.float32))
        low = jnp.minimum(low, got[k, 2].astype(jnp.float32))
    count = tally_ref[:, own_rows].astype(jnp.float32)
    full_rows = pl.ds(pl.multiple_of(margin + me * chunk, 16), chunk)
    full[:, full_rows] = ((total - high - low) / (count - 2.0)).astype(full.dtype)

    shares = []
    for k in range(1, n):
        copy = pltpu.make_async_remote_copy(
            src_ref=full.at[:, full_rows],
            dst_ref=full.at[:, full_rows],
            send_sem=sent_rows.at[k - 1],
            recv_sem=got_rows.at[k - 1],
            device_id=place(k)[1],
            device_id_type=MESH,
        )
        copy.start()
        shares.append(copy)
    for copy in copies:
        copy.wait_send()
    for copy in shares:
        copy.wait_recv()

    up = pltpu.make_async_remote_copy(
        src_ref=full.at[:, pl.ds(rows, margin)],
        dst_ref=full.at[:, pl.ds(0, margin)],
        send_sem=sent_edge.at[0],
        recv_sem=got_edge.at[0],
        device_id={"sky": lax.rem(sky + 1, patches)},
        device_id_type=MESH,
    )
    down = pltpu.make_async_remote_copy(
        src_ref=full.at[:, pl.ds(margin, margin)],
        dst_ref=full.at[:, pl.ds(rows + margin, margin)],
        send_sem=sent_edge.at[1],
        recv_sem=got_edge.at[1],
        device_id={"sky": lax.rem(sky + patches - 1, patches)},
        device_id_type=MESH,
    )

    @pl.when(has_high)
    def _():
        up.start()

    @pl.when(has_low)
    def _():
        down.start()

    side = lanes // 2
    out_ref[:, :side] = jnp.zeros((rows + 2 * margin, side), out_ref.dtype)
    out_ref[:, side + tiles * lanes :] = jnp.zeros((rows + 2 * margin, side), out_ref.dtype)

    def lay(row, count):
        image = jnp.concatenate([full[t, row : row + count] for t in range(tiles)], axis=1)
        out_ref[row : row + count, side : side + tiles * lanes] = image.astype(out_ref.dtype)

    lay(margin, rows)

    @pl.when(has_low)
    def _():
        up.wait_recv()

    @pl.when(has_high)
    def _():
        down.wait_recv()

    lay(0, margin)
    lay(rows + margin, margin)

    @pl.when(has_high)
    def _():
        up.wait_send()

    @pl.when(has_low)
    def _():
        down.wait_send()

    for copy in shares:
        copy.wait_send()


def padded_coadd(sizes, margin, partial_sums, partial_high, partial_low, tallies):
    tiles, rows, lanes = partial_sums.shape
    n = sizes[0] * sizes[1]
    return pl.pallas_call(
        functools.partial(coadd_kernel, sizes, margin),
        out_shape=jax.ShapeDtypeStruct((rows + 2 * margin, (tiles + 1) * lanes), jnp.float32),
        in_specs=[pl.BlockSpec(memory_space=pltpu.VMEM)] * 4,
        out_specs=pl.BlockSpec(memory_space=pltpu.VMEM),
        scratch_shapes=[
            pltpu.VMEM((n - 1, 3, tiles, rows // n, lanes), jnp.bfloat16),
            pltpu.VMEM((tiles, rows + 2 * margin, lanes), jnp.bfloat16),
            pltpu.SemaphoreType.DMA((n - 1, 3)),
            pltpu.SemaphoreType.DMA((n - 1, 3)),
            pltpu.SemaphoreType.DMA((n - 1,)),
            pltpu.SemaphoreType.DMA((n - 1,)),
            pltpu.SemaphoreType.DMA((2,)),
            pltpu.SemaphoreType.DMA((2,)),
        ],
        compiler_params=pltpu.CompilerParams(
            collective_id=1, has_side_effects=True, vmem_limit_bytes=24 * 2**20
        ),
    )(partial_sums, partial_high, partial_low, tallies)


def exchange_kernel(
    source_ref, warped_ref, label_ref, out_ref, out_label_ref,
    stage, landed, landed_labels, sent, received, sent_labels, received_labels,
):
    patches, capacity = stage.shape[:2]
    sky = lax.axis_index("sky")
    barrier = pltpu.get_barrier_semaphore()
    for k in range(1, patches):
        peer = lax.rem(sky + k, patches)
        pl.semaphore_signal(barrier, inc=1, device_id={"sky": peer}, device_id_type=MESH)
    for k in range(patches):
        block = lax.rem(sky + k, patches)
        for c in range(capacity):
            stage[k, c] = warped_ref[source_ref[block * capacity + c]]
    pl.semaphore_wait(barrier, patches - 1)
    copies = []
    for k in range(1, patches):
        peer = lax.rem(sky + k, patches)
        for src, dst, gone, come in (
            (stage.at[k], landed.at[k], sent, received),
            (label_ref.at[peer], landed_labels.at[k], sent_labels, received_labels),
        ):
            copy = pltpu.make_async_remote_copy(
                src_ref=src,
                dst_ref=dst,
                send_sem=gone.at[k],
                recv_sem=come.at[k],
                device_id={"sky": peer},
                device_id_type=MESH,
            )
            copy.start()
            copies.append(copy)
    out_ref[0] = stage[0]
    out_label_ref[0] = label_ref[sky]
    for i, copy in enumerate(copies):
        copy.wait_recv()
        k = i // 2 + 1
        if i % 2 == 0:
            out_ref[k] = landed[k]
        else:
            out_label_ref[k] = landed_labels[k]
    for copy in copies:
        copy.wait_send()


def exchange_tiles(sources, warped, labels):
    patches, capacity = labels.shape
    side = warped.shape[-1]
    spread = jnp.pad(
        labels.astype(jnp.bfloat16)[:, None, :], ((0, 0), (0, 15), (0, side - capacity))
    )
    vmem = pl.BlockSpec(memory_space=pltpu.VMEM)
    tiles = (patches, capacity, side, side)
    arrived, arrived_labels = pl.pallas_call(
        exchange_kernel,
        out_shape=(
            jax.ShapeDtypeStruct(tiles, jnp.bfloat16),
            jax.ShapeDtypeStruct(spread.shape, jnp.bfloat16),
        ),
        in_specs=[pl.BlockSpec(memory_space=pltpu.SMEM), vmem, vmem],
        out_specs=(vmem, vmem),
        scratch_shapes=[
            pltpu.VMEM(tiles, jnp.bfloat16),
            pltpu.VMEM(tiles, jnp.bfloat16),
            pltpu.VMEM(spread.shape, jnp.bfloat16),
            pltpu.SemaphoreType.DMA((patches,)),
            pltpu.SemaphoreType.DMA((patches,)),
            pltpu.SemaphoreType.DMA((patches,)),
            pltpu.SemaphoreType.DMA((patches,)),
        ],
        compiler_params=pltpu.CompilerParams(
            collective_id=2, has_side_effects=True, vmem_limit_bytes=32 * 2**20
        ),
    )(sources, warped, spread)
    return arrived, arrived_labels[:, 0, :capacity]


def place_kernel(seat_ref, arrived_ref, valid_ref, slab_ref, sum_ref, high_ref, low_ref):
    visit_count, tiles = slab_ref.shape[:2]

    def step(t, carry):
        total = high = low = None
        for v in range(visit_count):
            tile = arrived_ref[seat_ref[v * tiles + t]]
            slab_ref[v, t] = tile
            value = tile.astype(jnp.float32)
            usable = valid_ref[v, t].astype(jnp.float32)
            at_most = jnp.where(usable > 0.5, value, -jnp.inf)
            at_least = jnp.where(usable > 0.5, value, jnp.inf)
            if total is None:
                total, high, low = usable * value, at_most, at_least
            else:
                total = total + usable * value
                high, low = jnp.maximum(high, at_most), jnp.minimum(low, at_least)
        sum_ref[t] = total.astype(sum_ref.dtype)
        high_ref[t] = high.astype(high_ref.dtype)
        low_ref[t] = low.astype(low_ref.dtype)
        return carry

    lax.fori_loop(0, tiles, step, 0)


def place_tiles(seats, arrived, valid):
    visit_count, tiles, side, _ = valid.shape
    vmem = pl.BlockSpec(memory_space=pltpu.VMEM)
    plane = jax.ShapeDtypeStruct((tiles, side, side), jnp.bfloat16)
    return pl.pallas_call(
        place_kernel,
        out_shape=(jax.ShapeDtypeStruct(valid.shape, jnp.bfloat16), plane, plane, plane),
        in_specs=[pl.BlockSpec(memory_space=pltpu.SMEM), vmem, vmem],
        out_specs=(vmem,) * 4,
        compiler_params=pltpu.CompilerParams(vmem_limit_bytes=24 * 2**20),
    )(seats, arrived, valid)


def difference_kernel(basis_count, kernel_side, mix_ref, pad_ref, row_ref, slab_ref, valid_ref, out_ref, acc, turned):
    visit_count, tiles, side, _ = slab_ref.shape
    source = lax.broadcasted_iota(jnp.int32, (side, side), 0)
    target = lax.broadcasted_iota(jnp.int32, (side, side), 1)
    first, second = source > target, source < target

    def band_of(dy):
        upper, lower = [], []
        for b in range(basis_count):
            row = row_ref[pl.ds(dy * basis_count + b, 1), :]
            ring = pltpu.roll(
                jnp.broadcast_to(row, (side, side)), 0, axis=1, stride=1, stride_axis=0
            )
            upper.append(jnp.where(first, ring, 0.0).astype(jnp.bfloat16))
            lower.append(jnp.where(second, ring, 0.0).astype(jnp.bfloat16))
        return [jnp.concatenate(upper, axis=1), jnp.concatenate(lower, axis=1)]

    def windows_of(ref, r):
        shifted = ref[r : r + side, :].astype(jnp.bfloat16)
        return jnp.concatenate(
            [shifted[:, t * side : (t + 2) * side] for t in range(tiles)], axis=0
        )

    acc[...] = jnp.dot(
        windows_of(pad_ref, 0),
        jnp.concatenate(band_of(0), axis=0),
        preferred_element_type=jnp.float32,
    )
    height = pad_ref.shape[0]
    group = 8 if (kernel_side - 1) % 8 == 0 else 2

    def step(i, carry):
        dy = group * i + 1
        turned[...] = pltpu.roll(pad_ref[...], height - dy, axis=0)
        windows = jnp.concatenate([windows_of(turned, r) for r in range(group)], axis=1)
        band = jnp.concatenate([x for r in range(group) for x in band_of(dy + r)], axis=0)
        acc[...] += jnp.dot(windows, band, preferred_element_type=jnp.float32)
        return carry

    lax.fori_loop(0, (kernel_side - 1) // group, step, 0)

    for t in range(tiles):
        planes = [
            acc[t * side : (t + 1) * side, b * side : (b + 1) * side]
            .astype(jnp.bfloat16)
            .astype(jnp.float32)
            for b in range(basis_count)
        ]
        for v in range(visit_count):
            template = mix_ref[v, t * basis_count] * planes[0]
            for b in range(1, basis_count):
                template += mix_ref[v, t * basis_count + b] * planes[b]
            out_ref[v, :, t * side : (t + 1) * side] = (
                (slab_ref[v, t].astype(jnp.float32) - template)
                * valid_ref[v, t].astype(jnp.float32)
            ).astype(out_ref.dtype)


def filter_and_subtract(mixture, padded, kernels, slab_tiles, valid):
    visit_count, tiles, side, _ = slab_tiles.shape
    basis_count, kernel_side = kernels.shape[:2]
    margin = kernel_side // 2
    rows = jnp.pad(kernels.astype(jnp.float32), ((0, 0), (0, 0), (0, side - kernel_side)))
    rows = jnp.roll(jnp.flip(rows, axis=2), -(side // 2 - margin - 1), axis=2)
    rows = jnp.transpose(rows, (1, 0, 2)).reshape(kernel_side * basis_count, side)
    vmem = pl.BlockSpec(memory_space=pltpu.VMEM)
    return pl.pallas_call(
        functools.partial(difference_kernel, basis_count, kernel_side),
        out_shape=jax.ShapeDtypeStruct((visit_count, side, tiles * side), jnp.bfloat16),
        in_specs=[pl.BlockSpec(memory_space=pltpu.SMEM), vmem, vmem, vmem, vmem],
        out_specs=vmem,
        scratch_shapes=[
            pltpu.VMEM((tiles * side, basis_count * side), jnp.float32),
            pltpu.VMEM(padded.shape, jnp.float32),
        ],
        compiler_params=pltpu.CompilerParams(vmem_limit_bytes=48 * 2**20),
    )(mixture.reshape(visit_count, tiles * basis_count), padded, rows, slab_tiles, valid)


def on_device(
    raw_tiles,
    pixel_offsets,
    shift_entry_index,
    shift_table,
    tile_routes,
    bad_pixels,
    basis_kernels,
    basis_choice,
    coef_table,
):
    visit_count, tile_cols, tile_side = (raw_tiles.shape[0], raw_tiles.shape[1], raw_tiles.shape[2])
    patches = lax.axis_size("sky")
    pooled = visit_count * tile_cols
    capacity = (pooled + patches - 1) // patches + 1
    owners = (tile_routes // tile_cols).reshape(pooled)
    slots = (tile_routes % tile_cols + tile_cols * jnp.arange(visit_count)[:, None]).reshape(pooled)
    order = jnp.arange(pooled)
    earlier = (owners[None, :] == owners[:, None]) & (order[None, :] < order[:, None])
    seat_ids = owners * capacity + jnp.sum(earlier, axis=1)
    layout = seat_ids[None, :] == jnp.arange(patches * capacity)[:, None]
    sources = jnp.sum(jnp.where(layout, order[None, :], 0), axis=1)
    labels = jnp.sum(jnp.where(layout, slots[None, :] + 1, 0), axis=1) - 1
    warped = warp_tiles(raw_tiles, pixel_offsets, shift_entry_index, shift_table)
    arrived, arrived_labels = exchange_tiles(
        sources,
        warped.reshape(pooled, tile_side, tile_side),
        labels.reshape(patches, capacity),
    )
    landing = arrived_labels.astype(jnp.float32).reshape(1, -1) == order.astype(jnp.float32)[:, None]
    seats = jnp.sum(jnp.where(landing, jnp.arange(patches * capacity)[None, :], 0), axis=1)
    sizes = tuple(lax.axis_size(axis) for axis in ("visit", "band", "sky"))
    shard_index = lax.axis_index(("visit", "band"))
    visit_total = bad_pixels.shape[0]
    listed_count = bad_pixels.shape[2]
    own_listed = lax.dynamic_slice_in_dim(bad_pixels, shard_index * visit_count, visit_count, 0)
    valid_pixel_mask = 1.0 - hit_planes(own_listed, tile_side)
    all_listed = jnp.transpose(bad_pixels, (1, 0, 2)).reshape(
        tile_cols, visit_total * listed_count
    )
    tallies = (visit_total - hit_planes(all_listed, tile_side)).astype(jnp.bfloat16)
    valid = valid_pixel_mask.astype(jnp.bfloat16)
    slab_tiles, partial_sums, partial_high, partial_low = place_tiles(
        seats, arrived.reshape(patches * capacity, tile_side, tile_side), valid
    )
    margin = basis_kernels.shape[-1] // 2
    padded = padded_coadd(sizes, margin, partial_sums, partial_high, partial_low, tallies)
    entries = coef_table.shape[0]
    picks = (basis_choice[..., None] == jnp.arange(entries)).astype(jnp.float32)
    mixture = jnp.sum(picks[..., None] * coef_table, axis=2)
    return filter_and_subtract(
        mixture, padded, basis_kernels, slab_tiles, valid
    )


def solution(mesh):
    return jax.shard_map(
        on_device,
        mesh=mesh,
        in_specs=(
            P(("group", "visit", "band"), "sky", None, None),
            P(("group", "visit", "band"), "sky", None),
            P(("group", "visit", "band"), "sky"),
            P(),
            P(("group", "visit", "band"), "sky"),
            P("group", "sky", None),
            P(),
            P(("group", "visit", "band"), "sky"),
            P(),
        ),
        out_specs=P(("group", "visit", "band"), "sky", None),
        check_vma=False,
    )
```
